32 devices in a mesh: freq: 4 (over x, core), tile: 8 (over z, y).
Axes of the slice: x: 2, y: 2, z: 4, core: 2. Of those that a mesh axis runs over, the one named last changes fastest.
Arguments:
- model_field: bfloat16 [4, 4096, 256], P('freq', 'tile'), may hold values from -6 to 6
- data_field: bfloat16 [4, 4096, 256], P('freq', 'tile'), may hold values from -6 to 6
- u_codes: bfloat16 [4, 2, 4096, 704], P('freq', None, 'tile'), may hold values from -128 to 127, as said below
- u_scales: float32 [4, 8, 704], P('freq', 'tile'), as said below
- v_codes: bfloat16 [4, 2, 4096, 704], P('freq', None, 'tile'), may hold values from -128 to 127, as said below
- v_scales: float32 [4, 8, 704], P('freq', 'tile'), as said below
- tile_ranks: int32 [4, 8, 8], P('freq'), may hold values from 40 to 88, as said below
- mute_start: int32 [4096], P('tile'), may hold values from 0 to 64
Outputs:
- gradient_time: bfloat16 [4096, 128, 128], P('tile', 'freq')
The draws below stay inside these ranges and needn't reach their ends.
Inputs may be any that keep to these rules, and one draw needn't show every extreme that they name: `tile_ranks`: for every frequency the ranks are symmetric; one tile row (and column), drawn per frequency, has every tile of rank 88, so its total is exactly 704; no row or column totals more. `u_codes`: whole numbers. `v_codes`: whole numbers. `u_scales`: Positive. `v_scales`: Positive.
All inputs are finite; a program needn't handle non-finite values.
Results may differ from the reference program's by a relative error of at most 0.0075.
Values may be sent and summed in bfloat16 or wider, within the bound.
A program may use at most 128 MiB of HBM per device.

```python
import math
import jax
import jax.numpy as jnp
from jax import lax

B = 512
RSLOT = 88
RLO = 40
RHI = 80
S = 128
NTIME = 128
NT = 8
NF = 4
ORDER = 4096
CAP = 704


def code_table(key):
    whole = jax.random.randint(key, (NF, 2, ORDER, CAP), -128, 128, dtype=jnp.int32)
    return whole.astype(jnp.float32).astype(jnp.bfloat16)


def draw_u_codes(key, part):
    return code_table(jax.random.fold_in(key, 11))


def draw_v_codes(key, part):
    return code_table(jax.random.fold_in(key, 12))


def scale_table(key, base_std):
    low_end = math.log(0.3)
    high_end = math.log(3.0)
    spread = jax.random.uniform(key, (NF, NT, CAP), jnp.float32, low_end, high_end)
    return (jnp.exp(spread) * (base_std / 73.9)).astype(jnp.float32)


def draw_u_scales(key, part):
    return scale_table(jax.random.fold_in(key, 21), 1.0 / math.sqrt(CAP))


def draw_v_scales(key, part):
    return scale_table(jax.random.fold_in(key, 22), 1.0 / math.sqrt(2 * B))


def draw_tile_ranks(key, part):
    own_key = jax.random.fold_in(key, 31)
    base_key, pick_key = jax.random.split(own_key)
    base_draw = jax.random.randint(base_key, (NF, NT, NT), RLO, RHI + 1, dtype=jnp.int32)
    symmetric = jnp.triu(base_draw) + jnp.swapaxes(jnp.triu(base_draw, 1), 1, 2)
    heavy_row = jax.random.randint(pick_key, (NF,), 0, NT, dtype=jnp.int32)
    positions = jnp.arange(NT, dtype=jnp.int32)
    is_heavy = positions[None, :] == heavy_row[:, None]
    heavy_mask = is_heavy[:, :, None] | is_heavy[:, None, :]
    return jnp.where(heavy_mask, RSLOT, symmetric).astype(jnp.int32)


def place_ends(values, rng, smallest, top_value):
    longest = values.shape.index(max(values.shape))
    spots = []
    for shift in (0, 1):
        where = [jax.random.randint(jax.random.fold_in(rng, axis), (), 0, length) for axis, length in enumerate(values.shape)]
        where[longest] = (where[longest] + shift) % values.shape[longest]
        spots.append(tuple(where))
    return values.at[spots[0]].set(smallest).at[spots[1]].set(top_value)


def shard_levels(rng, extent, pieces, low, top_value):
    loudness, own = 1.0, jax.random.fold_in(rng, 6)
    for position, blocks in pieces:
        draws = jnp.exp(jax.random.uniform(jax.random.fold_in(own, position), (blocks,), jnp.float32, low / len(pieces), top_value / len(pieces)))
        loudness = loudness * jnp.repeat(draws, extent[position] // blocks).reshape([-1 if axis == position else 1 for axis in range(len(extent))])
    return loudness


def centred(rng, shape, deviation, limit, shards=(), kind=jnp.bfloat16):
    drawn = jax.random.normal(rng, shape, jnp.float32) * deviation
    if len(shards) > 0:
        drawn = shard_levels(rng, shape, shards, -0.22, 0.18) * drawn
    return jnp.clip(drawn, min=-limit, max=limit).astype(kind)


def setup_inputs(seed: int = 0) -> dict:
    keys = jax.random.split(jax.random.key(seed), 9)
    model_field = centred(keys[0], (NF, ORDER, 2 * S), 1.0, 6.0, ((0, 4), (1, 8)))
    data_field = centred(keys[1], (NF, ORDER, 2 * S), 1.0, 6.0, ((0, 4), (1, 8)))
    u_codes = draw_u_codes(jax.random.fold_in(keys[8], 71), 0)
    u_scales = draw_u_scales(jax.random.fold_in(keys[8], 71), 0)
    v_codes = draw_v_codes(jax.random.fold_in(keys[8], 71), 0)
    v_scales = draw_v_scales(jax.random.fold_in(keys[8], 71), 0)
    tile_ranks = draw_tile_ranks(jax.random.fold_in(keys[8], 71), 0)
    mute_start = place_ends(jax.random.randint(keys[7], (ORDER,), 0, NTIME // 2 + 1), jax.random.fold_in(keys[7], 1), 0, (NTIME // 2 + 1) - 1).astype(jnp.int32)
    return {"model_field": model_field, "data_field": data_field, "u_codes": u_codes, "u_scales": u_scales, "v_codes": v_codes, "v_scales": v_scales, "tile_ranks": tile_ranks, "mute_start": mute_start}


def unpack_pool(code_vals, scale_row):
    return (code_vals.astype(jnp.float32) * scale_row).astype(jnp.bfloat16)

def apply_factor(factor, pooled):
    half_width = pooled.shape[1] // 2
    real_part = jnp.dot(factor[0], pooled, preferred_element_type=jnp.float32)
    imag_part = jnp.dot(factor[1], pooled, preferred_element_type=jnp.float32)
    out_re = real_part[:, :half_width] - imag_part[:, half_width:]
    out_im = real_part[:, half_width:] + imag_part[:, :half_width]
    return jnp.concatenate([out_re, out_im], 1)

def apply_adjoint(factor, dense_rows):
    half_width = dense_rows.shape[1] // 2
    dims = (((0,), (0,)), ((), ()))
    real_part = lax.dot_general(factor[0], dense_rows, dims, preferred_element_type=jnp.float32)
    imag_part = lax.dot_general(factor[1], dense_rows, dims, preferred_element_type=jnp.float32)
    out_re = real_part[:, :half_width] + imag_part[:, half_width:]
    out_im = real_part[:, half_width:] - imag_part[:, :half_width]
    return jnp.concatenate([out_re, out_im], 1)

def pool_owner(ends, begins, capacity, tile_count):
    column = jnp.arange(capacity, dtype=jnp.int32)
    owner_raw = lax.optimization_barrier(jnp.sum((column[:, None] >= ends[None, :]).astype(jnp.int32), 1)).astype(jnp.int32)
    is_live = owner_raw < tile_count
    owner_tile = jnp.minimum(owner_raw, tile_count - 1).astype(jnp.int32)
    offset = (column - begins[owner_tile]).astype(jnp.int32)
    return (owner_tile, offset, is_live)

def reference(model_field, data_field, u_codes, u_scales, v_codes, v_scales, tile_ranks, mute_start):
    tile_count = NT
    capacity = CAP
    src_width = S

    def one_freq(freq_idx):
        rank_table = tile_ranks[freq_idx]
        row_end = jnp.cumsum(rank_table, 1).astype(jnp.int32)
        row_begin = (row_end - rank_table).astype(jnp.int32)
        col_end = jnp.cumsum(rank_table, 0).astype(jnp.int32)
        col_begin = (col_end - rank_table).astype(jnp.int32)
        model_f = model_field[freq_idx]
        data_f = data_field[freq_idx]
        ucodes_f = u_codes[freq_idx]
        vcodes_f = v_codes[freq_idx]
        uscale_f = u_scales[freq_idx]
        vscale_f = v_scales[freq_idx]

        def right_factor(col_tile):
            return unpack_pool(lax.dynamic_slice_in_dim(vcodes_f, col_tile * B, B, 1), vscale_f[col_tile])

        def column_pool(col_tile):
            factor = right_factor(col_tile)
            local_model = lax.dynamic_slice_in_dim(model_f, col_tile * B, B, 0)
            return apply_adjoint(factor, local_model).astype(jnp.bfloat16)
        tiles = jnp.arange(tile_count, dtype=jnp.int32)
        w_pools = lax.map(column_pool, tiles).reshape(tile_count * capacity, 2 * src_width)

        def row_section(row_tile):
            owner_tile, offset, is_live = pool_owner(row_end[row_tile], row_begin[row_tile], capacity, tile_count)
            source = owner_tile * capacity + col_begin[row_tile, owner_tile] + offset
            source = jnp.where(is_live, source, 0).astype(jnp.int32)
            pooled = jnp.where(is_live[:, None], w_pools[source], 0).astype(jnp.bfloat16)
            factor = unpack_pool(lax.dynamic_slice_in_dim(ucodes_f, row_tile * B, B, 1), uscale_f[row_tile])
            local_data = lax.dynamic_slice_in_dim(data_f, row_tile * B, B, 0).astype(jnp.float32)
            residual = (apply_factor(factor, pooled) - local_data).astype(jnp.bfloat16)
            return apply_adjoint(factor, residual).astype(jnp.bfloat16)
        p_pools = lax.map(row_section, tiles).reshape(tile_count * capacity, 2 * src_width)

        def column_grad(col_tile):
            owner_tile, offset, is_live = pool_owner(col_end[:, col_tile], col_begin[:, col_tile], capacity, tile_count)
            source = owner_tile * capacity + row_begin[owner_tile, col_tile] + offset
            source = jnp.where(is_live, source, 0).astype(jnp.int32)
            pooled = jnp.where(is_live[:, None], p_pools[source], 0).astype(jnp.bfloat16)
            return apply_factor(right_factor(col_tile), pooled).astype(jnp.bfloat16)
        return lax.map(column_grad, tiles).reshape(tile_count * B, 2 * src_width)
    spectra = lax.map(one_freq, jnp.arange(NF, dtype=jnp.int32))
    spectra = spectra.reshape(NF, tile_count * B, 2, src_width).astype(jnp.float32)
    freq_bin = jnp.arange(NF, dtype=jnp.int32).astype(jnp.float32) + 1.0
    time_grid = jnp.arange(NTIME, dtype=jnp.int32).astype(jnp.float32)
    phase_arg = 2.0 * math.pi * freq_bin[:, None] * time_grid[None, :] / NTIME
    time_basis = jnp.stack([jnp.cos(phase_arg), -jnp.sin(phase_arg)], 1)
    signal = 0.5 * jnp.einsum('fncs,fct->nst', spectra, time_basis, precision=lax.Precision.HIGHEST)
    unmuted = jnp.arange(NTIME, dtype=jnp.int32)[None, None, :] >= mute_start[:, None, None]
    return jnp.where(unmuted, signal, 0.0).astype(jnp.bfloat16)
```

```python
import functools
import math

import jax
import jax.numpy as jnp
import numpy as np
from jax import lax
from jax.experimental import pallas as pl
from jax.experimental.pallas import tpu as pltpu
from jax.sharding import PartitionSpec as P

NTIME = 128
HALVES = 2
BF = jnp.bfloat16
F32 = jnp.float32
MESH = pl.DeviceIdType.MESH
NT_DIMS = (((1,), (1,)), ((), ()))


def dot_nn(a, b):
    return jnp.dot(a, b, preferred_element_type=F32)


def dot_nt(a, b):
    return lax.dot_general(a, b, NT_DIMS, preferred_element_type=F32)


def exchange_kernel(
    tiles,
    freqs,
    ranks,
    model_hbm,
    data_hbm,
    ucodes_hbm,
    uscale,
    vcodes_hbm,
    vscale,
    out,
    model,
    data,
    ufac,
    vfac,
    sel,
    wt,
    uslot,
    uslot_t,
    vslot,
    dperm,
    pool,
    resid,
    sbuf,
    rbuf,
    fsend,
    frecv,
    load_sem,
    send_sem,
    recv_sem,
    fsend_sem,
    frecv_sem,
):
    tile = lax.axis_index("tile")
    freq = lax.axis_index("freq")
    rows, cols = model.shape
    lanes = cols // HALVES
    cap = ufac.shape[2]
    slot = cap // tiles
    pad = pool.shape[0] // tiles
    group = sel.shape[0] // pad
    groups = tiles // group
    part = lanes // freqs // 2
    brows = rows // freqs

    loads = [
        pltpu.make_async_copy(src, dst, load_sem.at[k])
        for k, (src, dst) in enumerate(
            [
                (model_hbm, model),
                (vcodes_hbm, vfac),
                (ucodes_hbm, ufac),
                (data_hbm, data),
            ]
        )
    ]
    for load in loads:
        load.start()

    barrier = pltpu.get_barrier_semaphore()
    for d in range(1, tiles):
        pl.semaphore_signal(
            barrier, inc=1, device_id=(freq, lax.rem(tile + d, tiles)), device_id_type=MESH
        )
    for d in range(1, freqs):
        pl.semaphore_signal(
            barrier, inc=1, device_id=(lax.rem(freq + d, freqs), tile), device_id_type=MESH
        )

    own = [ranks[i, tile] for i in range(tiles)]
    begins = []
    run = jnp.int32(0)
    for i in range(tiles):
        begins.append(run)
        run = run + own[i]

    def build_sel(g):
        k = lax.broadcasted_iota(jnp.int32, (pad, cap), 0)
        diff = lax.broadcasted_iota(jnp.int32, (pad, cap), 1) - k
        for b in range(group):
            i = g * group + b
            hit = (diff == begins[i]) & (k < own[i])
            sel[b * pad : (b + 1) * pad, :] = jnp.where(hit, 1.0, 0.0).astype(BF)

    def block_perm():
        p = lax.broadcasted_iota(jnp.int32, (cols, cols), 0)
        c = lax.broadcasted_iota(jnp.int32, (cols, cols), 1)
        half = p // lanes
        comp = (p % lanes) // (lanes // 2)
        share = (p % (lanes // 2)) // part
        nat = comp * (cols // 2) + share * (2 * part) + half * part + p % part
        return jnp.where(c == nat, 1.0, 0.0).astype(BF)

    build_sel(0)
    perm = block_perm()
    pool[...] = jnp.zeros_like(pool)
    loads[0].wait()
    mt = dot_nt(perm, model[...]).astype(BF)

    step = rows // 4

    def unpack(fac, scale):
        s = scale[...]

        def body(r, carry):
            for c in range(2):
                at = pl.ds(pl.multiple_of(r * step, step), step)
                fac[c, at, :] = (fac[c, at, :].astype(F32) * s).astype(BF)
            return carry

        lax.fori_loop(0, rows // step, body, 0)

    loads[1].wait()
    unpack(vfac, vscale)
    a = dot_nn(mt, vfac[0])
    b = dot_nn(mt, vfac[1])
    hl = lanes // 2
    for h in range(HALVES):
        o = h * lanes
        wt[o : o + hl, :] = (a[o : o + hl] + b[o + hl : o + lanes]).astype(BF)
        wt[o + hl : o + lanes, :] = (a[o + hl : o + lanes] - b[o : o + hl]).astype(BF)
    for g in range(groups):
        if groups > 1:
            build_sel(g)
        for h in range(HALVES):
            w = dot_nt(sel[...], wt[h * lanes : (h + 1) * lanes, :]).astype(BF)
            for k in range(group):
                sbuf[0, h, g * group + k] = w[k * pad : k * pad + slot]

    pl.semaphore_wait(barrier, tiles - 1 + freqs - 1)

    def block_copy(phase, h, d):
        dst = lax.rem(tile + d, tiles)
        return pltpu.make_async_remote_copy(
            src_ref=sbuf.at[phase, h, dst],
            dst_ref=rbuf.at[phase, h, tile],
            send_sem=send_sem.at[phase, h, dst],
            recv_sem=recv_sem.at[phase, h, tile],
            device_id=(freq, dst),
            device_id_type=MESH,
        )

    def block_arrival(phase, h, d):
        src = lax.rem(tile + d, tiles)
        return pltpu.make_async_remote_copy(
            src_ref=sbuf.at[phase, h, src],
            dst_ref=rbuf.at[phase, h, src],
            send_sem=send_sem.at[phase, h, src],
            recv_sem=recv_sem.at[phase, h, src],
            device_id=(freq, src),
            device_id_type=MESH,
        )

    def send_blocks(phase, h):
        for d in range(1, tiles):
            block_copy(phase, h, d).start()
        rbuf[phase, h, tile] = sbuf[phase, h, tile]

    def take_blocks(phase, h):
        for d in range(1, tiles):
            block_arrival(phase, h, d).wait_recv()
        for i in range(tiles):
            pool[i * pad : i * pad + slot, :] = rbuf[phase, h, i]

    send_blocks(0, 0)
    send_blocks(0, 1)

    lane = lax.broadcasted_iota(jnp.int32, (1, lanes), 1)
    sign = jnp.where(lane < hl, 1.0, -1.0).astype(F32)

    half_rows = rows // 2
    slots = pool.shape[0]
    srows = group * pad

    def to_slots(fac, slots_ref, slots_t_ref):
        for g in range(groups):
            if groups > 1:
                build_sel(g)

            for r in range(2):
                at = slice(r * half_rows, (r + 1) * half_rows)
                for c in range(2):
                    x = fac[c, at, :]
                    slots_ref[c, at, g * srows : (g + 1) * srows] = dot_nt(x, sel[...]).astype(BF)
                    if slots_t_ref is not None:
                        slots_t_ref[c, g * srows : (g + 1) * srows, at] = dot_nt(sel[...], x).astype(BF)

    loads[2].wait()
    unpack(ufac, uscale)
    to_slots(ufac, uslot, uslot_t)
    loads[3].wait()
    dperm[...] = dot_nt(data[...], perm)

    for h in range(HALVES):
        take_blocks(0, h)
        w = pool[...]
        re = dot_nn(uslot[0], w)
        im = dot_nn(uslot[1], w)
        y = re - sign * pltpu.roll(im, hl, 1)
        resid[...] = (y - dperm[:, h * lanes : (h + 1) * lanes]).astype(BF)
        x = resid[...]
        re = dot_nn(uslot_t[0], x)
        im = dot_nn(uslot_t[1], x)
        p = (re + sign * pltpu.roll(im, hl, 1)).astype(BF)
        for i in range(tiles):
            sbuf[1, h, i] = p[i * pad : i * pad + slot]
        send_blocks(1, h)
        if h == 0:
            to_slots(vfac, vslot, None)

    def swap_groups(pieces):
        out_pieces = []
        where_g = (lane % hl) // part
        for q in range(freqs):
            acc = pieces[0] if q == 0 else pltpu.roll(pieces[0], (lanes - q * part) % lanes, 1)
            for g in range(1, freqs):
                shift = (g - q) * part % lanes
                moved = pieces[g] if shift == 0 else pltpu.roll(pieces[g], shift, 1)
                acc = jnp.where(where_g == g, moved, acc)
            out_pieces.append(acc)
        return out_pieces

    def share_copy(h, d, arrival):
        other = lax.rem(freq + d, freqs)
        slot_at = other if arrival else freq
        return pltpu.make_async_remote_copy(
            src_ref=fsend.at[h, other],
            dst_ref=frecv.at[h, slot_at],
            send_sem=fsend_sem.at[h, other],
            recv_sem=frecv_sem.at[h, slot_at],
            device_id=(other, tile),
            device_id_type=MESH,
        )

    for h in range(HALVES):
        take_blocks(1, h)
        w = pool[...]
        re = dot_nn(vslot[0], w)
        im = dot_nn(vslot[1], w)
        grad = re - sign * pltpu.roll(im, hl, 1)
        packed = swap_groups([grad[g * brows : (g + 1) * brows] for g in range(freqs)])
        for q in range(freqs):
            fsend[h, q] = packed[q].astype(BF)
        for d in range(1, freqs):
            share_copy(h, d, False).start()
        frecv[h, freq] = fsend[h, freq]

    for h in range(HALVES):
        for d in range(1, freqs):
            share_copy(h, d, True).wait_recv()
        parts = swap_groups([frecv[h, f].astype(F32) for f in range(freqs)])
        for g in range(freqs):
            out[g * brows : (g + 1) * brows, h * lanes : (h + 1) * lanes] = parts[g]

    for h in range(HALVES):
        for phase in range(2):
            for d in range(1, tiles):
                block_copy(phase, h, d).wait_send()
        for d in range(1, freqs):
            share_copy(h, d, False).wait_send()


def time_kernel(share, freqs, mute, spec, basis, out):
    block = spec.shape[0]
    depth = spec.shape[1]
    start = pl.program_id(0) * block
    half = depth // HALVES
    part = share // HALVES
    s = lax.broadcasted_iota(jnp.int32, (share, depth), 0)
    k = lax.broadcasted_iota(jnp.int32, (share, depth), 1)
    keep = (k // half == s // part) & (k % part == s % part)
    mask = jnp.where(keep, 1.0, 0.0).astype(BF)
    table = basis[...]
    t = lax.broadcasted_iota(jnp.int32, (share, NTIME), 1)
    batch = 8
    for n0 in range(0, block, batch):
        rows = []
        for n in range(n0, n0 + batch):
            row = jnp.broadcast_to(spec[n : n + 1, :], (share, depth)).astype(BF)
            rows.append(row * mask)
        both = dot_nn(jnp.concatenate(rows, 0), table)
        signal = both[:, :NTIME] + both[:, NTIME:]
        for n in range(n0, n0 + batch):
            o = (n - n0) * share
            live = t >= mute[start + n]
            out[n] = jnp.where(live, signal[o : o + share], 0.0).astype(BF)


def time_table(freqs, share):
    part = share // HALVES
    k = np.arange(2 * share * freqs)
    f = (k % (part * freqs)) // part
    c = (k % (2 * part * freqs)) // (part * freqs)
    angle = 2.0 * math.pi * (f[:, None] + 1) * np.arange(NTIME)[None, :] / NTIME
    table = 0.5 * np.where(c[:, None] == 0, np.cos(angle), -np.sin(angle))
    high = table.astype(jnp.bfloat16)
    low = (table - high.astype(np.float64)).astype(jnp.bfloat16)
    return np.concatenate([high, low], 1)


def shards(tiles, freqs, model_field, data_field, u_codes, u_scales, v_codes, v_scales, tile_ranks, mute_start):
    rows, cols = model_field.shape[1:]
    cap = u_codes.shape[3]
    slot = cap // tiles
    pad = -(-slot // 32) * 32
    slots = tiles * pad
    group = min(tiles, 8)
    lanes = cols // HALVES
    share = cols // 2 // freqs
    brows = rows // freqs
    any_spec = pl.BlockSpec(memory_space=pl.ANY)
    vmem = pl.BlockSpec(memory_space=pltpu.VMEM)
    smem = pl.BlockSpec(memory_space=pltpu.SMEM)
    spectra = pl.pallas_call(
        functools.partial(exchange_kernel, tiles, freqs),
        out_shape=jax.ShapeDtypeStruct((rows, cols), F32),
        in_specs=[smem, any_spec, any_spec, any_spec, vmem, any_spec, vmem],
        out_specs=vmem,
        scratch_shapes=[
            pltpu.VMEM((rows, cols), BF),
            pltpu.VMEM((rows, cols), BF),
            pltpu.VMEM((2, rows, cap), BF),
            pltpu.VMEM((2, rows, cap), BF),
            pltpu.VMEM((group * pad, cap), BF),
            pltpu.VMEM((cols, cap), BF),
            pltpu.VMEM((2, rows, slots), BF),
            pltpu.VMEM((2, slots, rows), BF),
            pltpu.VMEM((2, rows, slots), BF),
            pltpu.VMEM((rows, cols), F32),
            pltpu.VMEM((slots, lanes), BF),
            pltpu.VMEM((rows, lanes), BF),
            pltpu.VMEM((2, HALVES, tiles, slot, lanes), BF),
            pltpu.VMEM((2, HALVES, tiles, slot, lanes), BF),
            pltpu.VMEM((HALVES, freqs, brows, lanes), BF),
            pltpu.VMEM((HALVES, freqs, brows, lanes), BF),
            pltpu.SemaphoreType.DMA((4,)),
            pltpu.SemaphoreType.DMA((2, HALVES, tiles)),
            pltpu.SemaphoreType.DMA((2, HALVES, tiles)),
            pltpu.SemaphoreType.DMA((HALVES, freqs)),
            pltpu.SemaphoreType.DMA((HALVES, freqs)),
        ],
        compiler_params=pltpu.CompilerParams(
            collective_id=0, has_side_effects=True, vmem_limit_bytes=60 * 2**20
        ),
        cost_estimate=pl.CostEstimate(
            flops=16 * rows * cap * cols, bytes_accessed=8 * rows * cap, transcendentals=0
        ),
        name="exchange",
    )(tile_ranks[0], model_field[0], data_field[0], u_codes[0], u_scales[0], v_codes[0], v_scales[0])
    table = jnp.asarray(time_table(freqs, share))
    block = 64
    return pl.pallas_call(
        functools.partial(time_kernel, share, freqs),
        out_shape=jax.ShapeDtypeStruct((rows, share, NTIME), BF),
        grid=(rows // block,),
        in_specs=[
            smem,
            pl.BlockSpec((block, cols), lambda i: (i, 0)),
            pl.BlockSpec((cols, 2 * NTIME), lambda i: (0, 0)),
        ],
        out_specs=pl.BlockSpec((block, share, NTIME), lambda i: (i, 0, 0)),
        compiler_params=pltpu.CompilerParams(vmem_limit_bytes=32 * 2**20),
        name="to_time",
    )(mute_start, spectra, table)


def solution(mesh):
    in_specs = (
        P("freq", "tile", None),
        P("freq", "tile", None),
        P("freq", None, "tile", None),
        P("freq", "tile", None),
        P("freq", None, "tile", None),
        P("freq", "tile", None),
        P("freq", None, None),
        P("tile"),
    )
    step = functools.partial(shards, mesh.shape["tile"], mesh.shape["freq"])
    return jax.shard_map(step, mesh=mesh, in_specs=in_specs, out_specs=P("tile", "freq", None), check_vma=False)
```

```python
import functools
import math

import jax
import jax.numpy as jnp
import numpy as np
from jax import lax
from jax.experimental import pallas as pl
from jax.experimental.pallas import tpu as pltpu
from jax.sharding import PartitionSpec as P

NTIME = 128
HALVES = 2
BF = jnp.bfloat16
F32 = jnp.float32
MESH = pl.DeviceIdType.MESH
NT_DIMS = (((1,), (1,)), ((), ()))


def dot_nn(a, b):
    return jnp.dot(a, b, preferred_element_type=F32)


def dot_nt(a, b):
    return lax.dot_general(a, b, NT_DIMS, preferred_element_type=F32)


def exchange_kernel(
    tiles,
    freqs,
    ranks,
    model_hbm,
    data_hbm,
    ucodes_hbm,
    uscale,
    vcodes_hbm,
    vscale,
    out,
    model,
    data,
    ufac,
    vfac,
    sel,
    wpool,
    eye,
    uslot,
    uslot_t,
    vslot,
    dperm,
    pool,
    resid,
    sbuf,
    rbuf,
    fsend,
    frecv,
    load_sem,
    send_sem,
    recv_sem,
    fsend_sem,
    frecv_sem,
):
    tile = lax.axis_index("tile")
    freq = lax.axis_index("freq")
    rows, cols = model.shape
    lanes = cols // HALVES
    cap = ufac.shape[1]
    slot = cap // tiles
    pad = pool.shape[0] // tiles
    group = sel.shape[0] // pad
    groups = tiles // group
    part = lanes // freqs // 2
    brows = rows // freqs

    loads = [
        pltpu.make_async_copy(src, dst, load_sem.at[k])
        for k, (src, dst) in enumerate(
            [
                (model_hbm, model),
                (vcodes_hbm, vfac),
                (ucodes_hbm, ufac),
                (data_hbm, data),
            ]
        )
    ]
    for load in loads:
        load.start()

    barrier = pltpu.get_barrier_semaphore()
    for d in range(1, tiles):
        pl.semaphore_signal(
            barrier, inc=1, device_id=(freq, lax.rem(tile + d, tiles)), device_id_type=MESH
        )
    for d in range(1, freqs):
        pl.semaphore_signal(
            barrier, inc=1, device_id=(lax.rem(freq + d, freqs), tile), device_id_type=MESH
        )

    own = [ranks[i, tile] for i in range(tiles)]
    begins = []
    run = jnp.int32(0)
    for i in range(tiles):
        begins.append(run)
        run = run + own[i]

    def build_sel(g):
        k = lax.broadcasted_iota(jnp.int32, (pad, cap), 0)
        diff = lax.broadcasted_iota(jnp.int32, (pad, cap), 1) - k
        for b in range(group):
            i = g * group + b
            hit = (diff == begins[i]) & (k < own[i])
            sel[b * pad : (b + 1) * pad, :] = jnp.where(hit, 1.0, 0.0).astype(BF)

    def block_perm():
        p = lax.broadcasted_iota(jnp.int32, (cols, cols), 0)
        c = lax.broadcasted_iota(jnp.int32, (cols, cols), 1)
        half = p // lanes
        comp = (p % lanes) // (lanes // 2)
        share = (p % (lanes // 2)) // part
        nat = comp * (cols // 2) + share * (2 * part) + half * part + p % part
        return jnp.where(c == nat, 1.0, 0.0).astype(BF)

    build_sel(0)
    perm = block_perm()
    pool[...] = jnp.zeros_like(pool)
    loads[0].wait()
    m = dot_nt(model[...], perm).astype(BF)

    step = 2 * slot

    def unpack(fac, scale):
        diff = lax.broadcasted_iota(jnp.int32, (step, cap), 1) - lax.broadcasted_iota(jnp.int32, (step, cap), 0)

        def body(r, carry):
            s = jnp.sum(jnp.where(diff == r * step, scale[...], 0.0), 1, keepdims=True)
            for c in range(2):
                at = pl.ds(pl.multiple_of(r * step, step), step)
                fac[c, at, :] = (fac[c, at, :].astype(F32) * s).astype(BF)
            return carry

        lax.fori_loop(0, cap // step, body, 0)

    loads[1].wait()
    unpack(vfac, vscale)
    hl = lanes // 2
    lane = lax.broadcasted_iota(jnp.int32, (1, lanes), 1)
    sign = jnp.where(lane < hl, 1.0, -1.0).astype(F32)
    a = dot_nn(vfac[0], m)
    b = dot_nn(vfac[1], m)
    for h in range(HALVES):
        at = slice(h * lanes, (h + 1) * lanes)
        wpool[:, at] = (a[:, at] + sign * pltpu.roll(b[:, at], hl, 1)).astype(BF)
    for g in range(groups):
        if groups > 1:
            build_sel(g)
        w = dot_nn(sel[...], wpool[...]).astype(BF)
        for h in range(HALVES):
            for k in range(group):
                sbuf[0, h, g * group + k] = w[k * pad : k * pad + slot, h * lanes : (h + 1) * lanes]

    pl.semaphore_wait(barrier, tiles - 1 + freqs - 1)

    def block_copy(phase, h, d):
        dst = lax.rem(tile + d, tiles)
        return pltpu.make_async_remote_copy(
            src_ref=sbuf.at[phase, h, dst],
            dst_ref=rbuf.at[phase, h, tile],
            send_sem=send_sem.at[phase, h, dst],
            recv_sem=recv_sem.at[phase, h, tile],
            device_id=(freq, dst),
            device_id_type=MESH,
        )

    def block_arrival(phase, h, d):
        src = lax.rem(tile + d, tiles)
        return pltpu.make_async_remote_copy(
            src_ref=sbuf.at[phase, h, src],
            dst_ref=rbuf.at[phase, h, src],
            send_sem=send_sem.at[phase, h, src],
            recv_sem=recv_sem.at[phase, h, src],
            device_id=(freq, src),
            device_id_type=MESH,
        )

    def send_blocks(phase, h):
        for d in range(1, tiles):
            block_copy(phase, h, d).start()
        rbuf[phase, h, tile] = sbuf[phase, h, tile]

    def take_blocks(phase, h):
        for d in range(1, tiles):
            block_arrival(phase, h, d).wait_recv()
        for i in range(tiles):
            pool[i * pad : i * pad + slot, :] = rbuf[phase, h, i]

    send_blocks(0, 0)
    send_blocks(0, 1)

    diag = lax.broadcasted_iota(jnp.int32, (rows, rows), 0) == lax.broadcasted_iota(jnp.int32, (rows, rows), 1)
    eye[...] = jnp.where(diag, 1.0, 0.0).astype(BF)
    srows = group * pad

    def to_slots(fac, slots_ref, slots_t_ref):
        for g in range(groups):
            if groups > 1:
                build_sel(g)

            at = slice(g * srows, (g + 1) * srows)
            for c in range(2):
                turned = dot_nn(sel[...], fac[c]).astype(BF)
                if slots_t_ref is not None:
                    slots_t_ref[c, at, :] = turned
                slots_ref[c, :, at] = dot_nt(eye[...], turned).astype(BF)

    loads[2].wait()
    unpack(ufac, uscale)
    to_slots(ufac, uslot, uslot_t)
    loads[3].wait()
    dperm[...] = dot_nt(data[...], perm)

    for h in range(HALVES):
        take_blocks(0, h)
        w = pool[...]
        re = dot_nn(uslot[0], w)
        im = dot_nn(uslot[1], w)
        y = re - sign * pltpu.roll(im, hl, 1)
        resid[...] = (y - dperm[:, h * lanes : (h + 1) * lanes]).astype(BF)
        x = resid[...]
        re = dot_nn(uslot_t[0], x)
        im = dot_nn(uslot_t[1], x)
        p = (re + sign * pltpu.roll(im, hl, 1)).astype(BF)
        for i in range(tiles):
            sbuf[1, h, i] = p[i * pad : i * pad + slot]
        send_blocks(1, h)
        if h == 0:
            to_slots(vfac, vslot, None)

    def swap_groups(pieces):
        out_pieces = []
        where_g = (lane % hl) // part
        for q in range(freqs):
            acc = pieces[0] if q == 0 else pltpu.roll(pieces[0], (lanes - q * part) % lanes, 1)
            for g in range(1, freqs):
                shift = (g - q) * part % lanes
                moved = pieces[g] if shift == 0 else pltpu.roll(pieces[g], shift, 1)
                acc = jnp.where(where_g == g, moved, acc)
            out_pieces.append(acc)
        return out_pieces

    def share_copy(h, d, arrival):
        other = lax.rem(freq + d, freqs)
        slot_at = other if arrival else freq
        return pltpu.make_async_remote_copy(
            src_ref=fsend.at[h, other],
            dst_ref=frecv.at[h, slot_at],
            send_sem=fsend_sem.at[h, other],
            recv_sem=frecv_sem.at[h, slot_at],
            device_id=(other, tile),
            device_id_type=MESH,
        )

    for h in range(HALVES):
        take_blocks(1, h)
        w = pool[...]
        re = dot_nn(vslot[0], w)
        im = dot_nn(vslot[1], w)
        grad = re - sign * pltpu.roll(im, hl, 1)
        packed = swap_groups([grad[g * brows : (g + 1) * brows] for g in range(freqs)])
        for q in range(freqs):
            fsend[h, q] = packed[q].astype(BF)
        for d in range(1, freqs):
            share_copy(h, d, False).start()
        frecv[h, freq] = fsend[h, freq]

    for h in range(HALVES):
        for d in range(1, freqs):
            share_copy(h, d, True).wait_recv()
        parts = swap_groups([frecv[h, f].astype(F32) for f in range(freqs)])
        for g in range(freqs):
            out[g * brows : (g + 1) * brows, h * lanes : (h + 1) * lanes] = parts[g].astype(BF)

    for h in range(HALVES):
        for phase in range(2):
            for d in range(1, tiles):
                block_copy(phase, h, d).wait_send()
        for d in range(1, freqs):
            share_copy(h, d, False).wait_send()


def time_kernel(share, freqs, mute, spec, basis, out):
    block = spec.shape[0]
    depth = spec.shape[1]
    start = pl.program_id(0) * block
    half = depth // HALVES
    part = share // HALVES
    s = lax.broadcasted_iota(jnp.int32, (part, half), 0)
    k = lax.broadcasted_iota(jnp.int32, (part, half), 1)
    keep = k % part == s
    table = basis[...]
    t = lax.broadcasted_iota(jnp.int32, (part, NTIME), 1)
    batch = 16
    for n0 in range(0, block, batch):
        g = spec[n0 : n0 + batch, :].astype(F32)
        rows = []
        for n in range(0, batch, 2):
            for h in range(HALVES):
                at = slice(h * half, (h + 1) * half)
                pair = [
                    jnp.where(keep, jnp.broadcast_to(g[n + e : n + e + 1, at], (part, half)), 0.0).astype(BF)
                    for e in range(2)
                ]
                rows.append(jnp.concatenate(pair, 1))
        signal = dot_nn(jnp.concatenate(rows, 0), table)
        for n in range(batch):
            live = t >= mute[start + n0 + n]
            e = n % 2
            for h in range(HALVES):
                o = ((n // 2) * HALVES + h) * part
                piece = signal[o : o + part, e * NTIME : (e + 1) * NTIME]
                out[n0 + n, h * part : (h + 1) * part, :] = jnp.where(live, piece, 0.0).astype(BF)


def time_table(freqs, share):
    part = share // HALVES
    k = np.arange(share * freqs)
    f = (k % (part * freqs)) // part
    c = k // (part * freqs)
    angle = 2.0 * math.pi * (f[:, None] + 1) * np.arange(NTIME)[None, :] / NTIME
    table = 0.5 * np.where(c[:, None] == 0, np.cos(angle), -np.sin(angle))
    return np.kron(np.eye(2), table).astype(jnp.bfloat16)


def shards(tiles, freqs, model_field, data_field, u_codes, u_scales, v_codes, v_scales, tile_ranks, mute_start):
    rows, cols = model_field.shape[1:]
    cap = u_codes.shape[3]
    u_turned = jnp.swapaxes(u_codes[0], 1, 2)
    v_turned = jnp.swapaxes(v_codes[0], 1, 2)
    slot = cap // tiles
    pad = -(-slot // 32) * 32
    slots = tiles * pad
    group = min(tiles, 8)
    lanes = cols // HALVES
    share = cols // 2 // freqs
    brows = rows // freqs
    any_spec = pl.BlockSpec(memory_space=pl.ANY)
    vmem = pl.BlockSpec(memory_space=pltpu.VMEM)
    smem = pl.BlockSpec(memory_space=pltpu.SMEM)
    spectra = pl.pallas_call(
        functools.partial(exchange_kernel, tiles, freqs),
        out_shape=jax.ShapeDtypeStruct((rows, cols), BF),
        in_specs=[smem, any_spec, any_spec, any_spec, vmem, any_spec, vmem],
        out_specs=vmem,
        scratch_shapes=[
            pltpu.VMEM((rows, cols), BF),
            pltpu.VMEM((rows, cols), BF),
            pltpu.VMEM((2, cap, rows), BF),
            pltpu.VMEM((2, cap, rows), BF),
            pltpu.VMEM((group * pad, cap), BF),
            pltpu.VMEM((cap, cols), BF),
            pltpu.VMEM((rows, rows), BF),
            pltpu.VMEM((2, rows, slots), BF),
            pltpu.VMEM((2, slots, rows), BF),
            pltpu.VMEM((2, rows, slots), BF),
            pltpu.VMEM((rows, cols), F32),
            pltpu.VMEM((slots, lanes), BF),
            pltpu.VMEM((rows, lanes), BF),
            pltpu.VMEM((2, HALVES, tiles, slot, lanes), BF),
            pltpu.VMEM((2, HALVES, tiles, slot, lanes), BF),
            pltpu.VMEM((HALVES, freqs, brows, lanes), BF),
            pltpu.VMEM((HALVES, freqs, brows, lanes), BF),
            pltpu.SemaphoreType.DMA((4,)),
            pltpu.SemaphoreType.DMA((2, HALVES, tiles)),
            pltpu.SemaphoreType.DMA((2, HALVES, tiles)),
            pltpu.SemaphoreType.DMA((HALVES, freqs)),
            pltpu.SemaphoreType.DMA((HALVES, freqs)),
        ],
        compiler_params=pltpu.CompilerParams(
            collective_id=0, has_side_effects=True, vmem_limit_bytes=60 * 2**20
        ),
        cost_estimate=pl.CostEstimate(
            flops=16 * rows * cap * cols, bytes_accessed=8 * rows * cap, transcendentals=0
        ),
        name="exchange",
    )(tile_ranks[0], model_field[0], data_field[0], u_turned, u_scales[0], v_turned, v_scales[0])
    table = jnp.asarray(time_table(freqs, share))
    block = 64
    return pl.pallas_call(
        functools.partial(time_kernel, share, freqs),
        out_shape=jax.ShapeDtypeStruct((rows, share, NTIME), BF),
        grid=(rows // block,),
        in_specs=[
            smem,
            pl.BlockSpec((block, cols), lambda i: (i, 0)),
            pl.BlockSpec((cols, 2 * NTIME), lambda i: (0, 0)),
        ],
        out_specs=pl.BlockSpec((block, share, NTIME), lambda i: (i, 0, 0)),
        compiler_params=pltpu.CompilerParams(vmem_limit_bytes=32 * 2**20),
        name="to_time",
    )(mute_start, spectra, table)


def solution(mesh):
    in_specs = (
        P("freq", "tile", None),
        P("freq", "tile", None),
        P("freq", None, "tile", None),
        P("freq", "tile", None),
        P("freq", None, "tile", None),
        P("freq", "tile", None),
        P("freq", None, None),
        P("tile"),
    )
    step = functools.partial(shards, mesh.shape["tile"], mesh.shape["freq"])
    return jax.shard_map(step, mesh=mesh, in_specs=in_specs, out_specs=P("tile", "freq", None), check_vma=False)
```

```python
import functools
import math

import jax
import jax.numpy as jnp
import numpy as np
from jax import lax
from jax.experimental import pallas as pl
from jax.experimental.pallas import tpu as pltpu
from jax.sharding import PartitionSpec as P

NTIME = 128
HALVES = 2
BF = jnp.bfloat16
F32 = jnp.float32
MESH = pl.DeviceIdType.MESH
NT_DIMS = (((1,), (1,)), ((), ()))


def dot_nn(a, b):
    return jnp.dot(a, b, preferred_element_type=F32)


def dot_nt(a, b):
    return lax.dot_general(a, b, NT_DIMS, preferred_element_type=F32)


def exchange_kernel(
    tiles,
    freqs,
    ranks,
    model_hbm,
    data_hbm,
    ucodes_hbm,
    uscale,
    vcodes_hbm,
    vscale,
    out,
    model,
    data,
    ufac,
    vfac,
    sel,
    wpool,
    eye,
    uslot,
    uslot_t,
    vslot,
    dperm,
    pool,
    resid,
    sbuf,
    rbuf,
    fsend,
    frecv,
    load_sem,
    send_sem,
    recv_sem,
    fsend_sem,
    frecv_sem,
):
    tile = lax.axis_index("tile")
    freq = lax.axis_index("freq")
    rows, cols = model.shape
    lanes = cols // HALVES
    cap = ufac.shape[1]
    slot = cap // tiles
    pad = pool.shape[0] // tiles
    group = sel.shape[0] // pad
    groups = tiles // group
    part = lanes // freqs // 2
    brows = rows // freqs

    loads = [
        pltpu.make_async_copy(src, dst, load_sem.at[k])
        for k, (src, dst) in enumerate(
            [
                (model_hbm, model),
                (vcodes_hbm, vfac),
                (ucodes_hbm, ufac),
                (data_hbm, data),
            ]
        )
    ]
    for load in loads:
        load.start()

    barrier = pltpu.get_barrier_semaphore()
    for d in range(1, tiles):
        pl.semaphore_signal(
            barrier, inc=1, device_id=(freq, lax.rem(tile + d, tiles)), device_id_type=MESH
        )
    for d in range(1, freqs):
        pl.semaphore_signal(
            barrier, inc=1, device_id=(lax.rem(freq + d, freqs), tile), device_id_type=MESH
        )

    own = [ranks[i, tile] for i in range(tiles)]
    begins = []
    run = jnp.int32(0)
    for i in range(tiles):
        begins.append(run)
        run = run + own[i]

    def build_sel(g):
        k = lax.broadcasted_iota(jnp.int32, (pad, cap), 0)
        diff = lax.broadcasted_iota(jnp.int32, (pad, cap), 1) - k
        for b in range(group):
            i = g * group + b
            hit = (diff == begins[i]) & (k < own[i])
            sel[b * pad : (b + 1) * pad, :] = jnp.where(hit, 1.0, 0.0).astype(BF)

    def block_perm():
        p = lax.broadcasted_iota(jnp.int32, (cols, cols), 0)
        c = lax.broadcasted_iota(jnp.int32, (cols, cols), 1)
        half = p // lanes
        comp = (p % lanes) // (lanes // 2)
        share = (p % (lanes // 2)) // part
        nat = comp * (cols // 2) + share * (2 * part) + half * part + p % part
        return jnp.where(c == nat, 1.0, 0.0).astype(BF)

    build_sel(0)
    perm = block_perm()
    pool[...] = jnp.zeros_like(pool)
    loads[0].wait()
    m = dot_nt(model[...], perm).astype(BF)

    step = 2 * slot

    def unpack(fac, scale):
        diff = lax.broadcasted_iota(jnp.int32, (step, cap), 1) - lax.broadcasted_iota(jnp.int32, (step, cap), 0)

        def body(r, carry):
            s = jnp.sum(jnp.where(diff == r * step, scale[...], 0.0), 1, keepdims=True)
            for c in range(2):
                at = pl.ds(pl.multiple_of(r * step, step), step)
                fac[c, at, :] = (fac[c, at, :].astype(F32) * s).astype(BF)
            return carry

        lax.fori_loop(0, cap // step, body, 0)

    loads[1].wait()
    unpack(vfac, vscale)
    hl = lanes // 2
    lane = lax.broadcasted_iota(jnp.int32, (1, lanes), 1)
    sign = jnp.where(lane < hl, 1.0, -1.0).astype(F32)
    a = dot_nn(vfac[0], m)
    b = dot_nn(vfac[1], m)
    for h in range(HALVES):
        at = slice(h * lanes, (h + 1) * lanes)
        wpool[:, at] = (a[:, at] + sign * pltpu.roll(b[:, at], hl, 1)).astype(BF)
    for g in range(groups):
        if groups > 1:
            build_sel(g)
        w = dot_nn(sel[...], wpool[...]).astype(BF)
        for h in range(HALVES):
            for k in range(group):
                sbuf[0, h, g * group + k] = w[k * pad : k * pad + slot, h * lanes : (h + 1) * lanes]

    pl.semaphore_wait(barrier, tiles - 1 + freqs - 1)

    def block_copy(phase, h, d):
        dst = lax.rem(tile + d, tiles)
        return pltpu.make_async_remote_copy(
            src_ref=sbuf.at[phase, h, dst],
            dst_ref=rbuf.at[phase, h, tile],
            send_sem=send_sem.at[phase, h, dst],
            recv_sem=recv_sem.at[phase, h, tile],
            device_id=(freq, dst),
            device_id_type=MESH,
        )

    def block_arrival(phase, h, d):
        src = lax.rem(tile + d, tiles)
        return pltpu.make_async_remote_copy(
            src_ref=sbuf.at[phase, h, src],
            dst_ref=rbuf.at[phase, h, src],
            send_sem=send_sem.at[phase, h, src],
            recv_sem=recv_sem.at[phase, h, src],
            device_id=(freq, src),
            device_id_type=MESH,
        )

    def send_blocks(phase, h):
        for d in range(1, tiles):
            block_copy(phase, h, d).start()
        rbuf[phase, h, tile] = sbuf[phase, h, tile]

    def take_blocks(phase, h):
        for d in range(1, tiles):
            block_arrival(phase, h, d).wait_recv()
        for i in range(tiles):
            pool[i * pad : i * pad + slot, :] = rbuf[phase, h, i]

    send_blocks(0, 0)
    send_blocks(0, 1)

    diag = lax.broadcasted_iota(jnp.int32, (rows, rows), 0) == lax.broadcasted_iota(jnp.int32, (rows, rows), 1)
    eye[...] = jnp.where(diag, 1.0, 0.0).astype(BF)
    srows = group * pad

    def to_slots(fac, slots_ref, slots_t_ref):
        for g in range(groups):
            if groups > 1:
                build_sel(g)

            at = slice(g * srows, (g + 1) * srows)
            for c in range(2):
                turned = dot_nn(sel[...], fac[c]).astype(BF)
                if slots_t_ref is not None:
                    slots_t_ref[c, at, :] = turned
                slots_ref[c, :, at] = dot_nt(eye[...], turned).astype(BF)

    loads[2].wait()
    unpack(ufac, uscale)
    to_slots(ufac, uslot, uslot_t)
    loads[3].wait()
    dperm[...] = dot_nt(data[...], perm)

    for h in range(HALVES):
        take_blocks(0, h)
        w = pool[...]
        re = dot_nn(uslot[0], w)
        im = dot_nn(uslot[1], w)
        y = re - sign * pltpu.roll(im, hl, 1)
        resid[...] = (y - dperm[:, h * lanes : (h + 1) * lanes]).astype(BF)
        x = resid[...]
        re = dot_nn(uslot_t[0], x)
        im = dot_nn(uslot_t[1], x)
        p = (re + sign * pltpu.roll(im, hl, 1)).astype(BF)
        for i in range(tiles):
            sbuf[1, h, i] = p[i * pad : i * pad + slot]
        send_blocks(1, h)
    to_slots(vfac, vslot, None)

    def swap_groups(pieces):
        out_pieces = []
        where_g = (lane % hl) // part
        for q in range(freqs):
            acc = pieces[0] if q == 0 else pltpu.roll(pieces[0], (lanes - q * part) % lanes, 1)
            for g in range(1, freqs):
                shift = (g - q) * part % lanes
                moved = pieces[g] if shift == 0 else pltpu.roll(pieces[g], shift, 1)
                acc = jnp.where(where_g == g, moved, acc)
            out_pieces.append(acc)
        return out_pieces

    def share_copy(h, d, arrival):
        other = lax.rem(freq + d, freqs)
        slot_at = other if arrival else freq
        return pltpu.make_async_remote_copy(
            src_ref=fsend.at[h, other],
            dst_ref=frecv.at[h, slot_at],
            send_sem=fsend_sem.at[h, other],
            recv_sem=frecv_sem.at[h, slot_at],
            device_id=(other, tile),
            device_id_type=MESH,
        )

    for h in range(HALVES):
        take_blocks(1, h)
        w = pool[...]
        re = dot_nn(vslot[0], w)
        im = dot_nn(vslot[1], w)
        grad = re - sign * pltpu.roll(im, hl, 1)
        packed = swap_groups([grad[g * brows : (g + 1) * brows] for g in range(freqs)])
        for q in range(freqs):
            fsend[h, q] = packed[q].astype(BF)
        for d in range(1, freqs):
            share_copy(h, d, False).start()
        frecv[h, freq] = fsend[h, freq]

    for h in range(HALVES):
        for d in range(1, freqs):
            share_copy(h, d, True).wait_recv()
        parts = swap_groups([frecv[h, f].astype(F32) for f in range(freqs)])
        for g in range(freqs):
            out[g * brows : (g + 1) * brows, h * lanes : (h + 1) * lanes] = parts[g].astype(BF)

    for h in range(HALVES):
        for phase in range(2):
            for d in range(1, tiles):
                block_copy(phase, h, d).wait_send()
        for d in range(1, freqs):
            share_copy(h, d, False).wait_send()


def time_kernel(share, freqs, mute, spec, basis, out):
    block = spec.shape[0]
    depth = spec.shape[1]
    start = pl.program_id(0) * block
    half = depth // HALVES
    part = share // HALVES
    s = lax.broadcasted_iota(jnp.int32, (part, half), 0)
    k = lax.broadcasted_iota(jnp.int32, (part, half), 1)
    keep = k % part == s
    table = basis[...]
    t = lax.broadcasted_iota(jnp.int32, (part, NTIME), 1)
    batch = block
    for n0 in range(0, block, batch):
        g = spec[n0 : n0 + batch, :].astype(F32)
        rows = []
        for n in range(0, batch, 2):
            for h in range(HALVES):
                at = slice(h * half, (h + 1) * half)
                pair = [
                    jnp.where(keep, jnp.broadcast_to(g[n + e : n + e + 1, at], (part, half)), 0.0).astype(BF)
                    for e in range(2)
                ]
                rows.append(jnp.concatenate(pair, 1))
        signal = dot_nn(jnp.concatenate(rows, 0), table)
        for n in range(batch):
            live = t >= mute[start + n0 + n]
            e = n % 2
            for h in range(HALVES):
                o = ((n // 2) * HALVES + h) * part
                piece = signal[o : o + part, e * NTIME : (e + 1) * NTIME]
                out[n0 + n, h * part : (h + 1) * part, :] = jnp.where(live, piece, 0.0).astype(BF)


def time_table(freqs, share):
    part = share // HALVES
    k = np.arange(share * freqs)
    f = (k % (part * freqs)) // part
    c = k // (part * freqs)
    angle = 2.0 * math.pi * (f[:, None] + 1) * np.arange(NTIME)[None, :] / NTIME
    table = 0.5 * np.where(c[:, None] == 0, np.cos(angle), -np.sin(angle))
    return np.kron(np.eye(2), table).astype(jnp.bfloat16)


def shards(tiles, freqs, model_field, data_field, u_codes, u_scales, v_codes, v_scales, tile_ranks, mute_start):
    rows, cols = model_field.shape[1:]
    cap = u_codes.shape[3]
    u_turned = jnp.swapaxes(u_codes[0], 1, 2)
    v_turned = jnp.swapaxes(v_codes[0], 1, 2)
    slot = cap // tiles
    pad = -(-slot // 32) * 32
    slots = tiles * pad
    group = min(tiles, 8)
    lanes = cols // HALVES
    share = cols // 2 // freqs
    brows = rows // freqs
    any_spec = pl.BlockSpec(memory_space=pl.ANY)
    vmem = pl.BlockSpec(memory_space=pltpu.VMEM)
    smem = pl.BlockSpec(memory_space=pltpu.SMEM)
    spectra = pl.pallas_call(
        functools.partial(exchange_kernel, tiles, freqs),
        out_shape=jax.ShapeDtypeStruct((rows, cols), BF),
        in_specs=[smem, any_spec, any_spec, any_spec, vmem, any_spec, vmem],
        out_specs=vmem,
        scratch_shapes=[
            pltpu.VMEM((rows, cols), BF),
            pltpu.VMEM((rows, cols), BF),
            pltpu.VMEM((2, cap, rows), BF),
            pltpu.VMEM((2, cap, rows), BF),
            pltpu.VMEM((group * pad, cap), BF),
            pltpu.VMEM((cap, cols), BF),
            pltpu.VMEM((rows, rows), BF),
            pltpu.VMEM((2, rows, slots), BF),
            pltpu.VMEM((2, slots, rows), BF),
            pltpu.VMEM((2, rows, slots), BF),
            pltpu.VMEM((rows, cols), F32),
            pltpu.VMEM((slots, lanes), BF),
            pltpu.VMEM((rows, lanes), BF),
            pltpu.VMEM((2, HALVES, tiles, slot, lanes), BF),
            pltpu.VMEM((2, HALVES, tiles, slot, lanes), BF),
            pltpu.VMEM((HALVES, freqs, brows, lanes), BF),
            pltpu.VMEM((HALVES, freqs, brows, lanes), BF),
            pltpu.SemaphoreType.DMA((4,)),
            pltpu.SemaphoreType.DMA((2, HALVES, tiles)),
            pltpu.SemaphoreType.DMA((2, HALVES, tiles)),
            pltpu.SemaphoreType.DMA((HALVES, freqs)),
            pltpu.SemaphoreType.DMA((HALVES, freqs)),
        ],
        compiler_params=pltpu.CompilerParams(
            collective_id=0, has_side_effects=True, vmem_limit_bytes=60 * 2**20
        ),
        cost_estimate=pl.CostEstimate(
            flops=16 * rows * cap * cols, bytes_accessed=8 * rows * cap, transcendentals=0
        ),
        name="exchange",
    )(tile_ranks[0], model_field[0], data_field[0], u_turned, u_scales[0], v_turned, v_scales[0])
    table = jnp.asarray(time_table(freqs, share))
    block = 64
    return pl.pallas_call(
        functools.partial(time_kernel, share, freqs),
        out_shape=jax.ShapeDtypeStruct((rows, share, NTIME), BF),
        grid=(rows // block,),
        in_specs=[
            smem,
            pl.BlockSpec((block, cols), lambda i: (i, 0)),
            pl.BlockSpec((cols, 2 * NTIME), lambda i: (0, 0)),
        ],
        out_specs=pl.BlockSpec((block, share, NTIME), lambda i: (i, 0, 0)),
        compiler_params=pltpu.CompilerParams(vmem_limit_bytes=32 * 2**20),
        name="to_time",
    )(mute_start, spectra, table)


def solution(mesh):
    in_specs = (
        P("freq", "tile", None),
        P("freq", "tile", None),
        P("freq", None, "tile", None),
        P("freq", "tile", None),
        P("freq", None, "tile", None),
        P("freq", "tile", None),
        P("freq", None, None),
        P("tile"),
    )
    step = functools.partial(shards, mesh.shape["tile"], mesh.shape["freq"])
    return jax.shard_map(step, mesh=mesh, in_specs=in_specs, out_specs=P("tile", "freq", None), check_vma=False)
```
